256 devices in a mesh: hi: 16 (over y, z_hi, core), lo: 16 (over z_lo, x).
Axes of the slice: x: 4, y: 4, z: 8 (z_hi: 2, z_lo: 4; z = z_hi * 4 + z_lo), core: 2. Of those that a mesh axis runs over, the one named last changes fastest.
Arguments:
- inputs: bfloat16 [131072, 192], P(('hi', 'lo')), may hold values from -6 to 6
- upstream: bfloat16 [131072, 192], P(('hi', 'lo')), may hold values from -6 to 6
- w_in: bfloat16 [768, 384], replicated, may hold values from -0.3125 to 0.3125
- w_out: bfloat16 [768, 384], replicated, may hold values from -0.21875 to 0.21875
- bias: float32 [768], replicated, may hold values from -4 to 4
Outputs:
- features_out: bfloat16 [131072, 192], P(('hi', 'lo'))
- grad_input: bfloat16 [131072, 192], P(('hi', 'lo'))
- grad_w_in: float32 [768, 384], P(('hi', 'lo'))
- grad_w_out: float32 [768, 384], P(('hi', 'lo'))
- grad_bias: float32 [768], P(('hi', 'lo'))
The draws below stay inside these ranges and needn't reach their ends.
All inputs are finite; a program needn't handle non-finite values.
Results may differ from the reference program's by a relative error of at most 0.015.
Values may be sent and summed in bfloat16 or wider, within the bound.
No kernel may reach another device: no remote copies, remote signals or barrier semaphores. Data moves between devices by JAX's collectives and lax.ppermute only.
A program may use at most 64 MiB of HBM per device.

```python
import math
import jax
import jax.numpy as jnp
from jax import lax

M = 192
H = 768
ROWS = 512
TOKENS = 131072
N_HI = 16
N_LO = 16


def levels(own_key, extent, pieces, low, top_value):
    gain, own = 1.0, jax.random.fold_in(own_key, 6)
    for axis_at, parts in pieces:
        steps = jnp.exp(jax.random.uniform(jax.random.fold_in(own, axis_at), (parts,), jnp.float32, low / len(pieces), top_value / len(pieces)))
        gain = gain * jnp.repeat(steps, extent[axis_at] // parts).reshape([-1 if axis == axis_at else 1 for axis in range(len(extent))])
    return gain


def centred(stream_key, shape, scale, bound, pieces=(), held_as=jnp.bfloat16):
    drawn = scale * jax.random.normal(stream_key, shape, jnp.float32)
    if pieces:
        drawn = drawn * levels(stream_key, shape, pieces, -0.22, 0.18)
    return jnp.clip(drawn, -bound, bound).astype(held_as)


def setup_inputs(seed: int = 0) -> dict:
    key_list = jax.random.split(jax.random.key(seed), 6)
    inputs = centred(key_list[0], (TOKENS, M), 1.0, 6.0, ((0, 256),))
    upstream = centred(key_list[1], (TOKENS, M), 1.0, 6.0, ((0, 256),))
    w_in = centred(key_list[2], (H, 2 * M), (2 * M) ** -0.5, 0.3125)
    w_out = centred(key_list[3], (H, 2 * M), H ** -0.5, 0.21875)
    bias = centred(key_list[4], (H,), 1.0, 4.0, (), jnp.float32)
    return dict(inputs=inputs, upstream=upstream, w_in=w_in, w_out=w_out, bias=bias)


def bit_count(value):
    return value.bit_length() - 1

def gelu_pair(pre):
    coeff = math.sqrt(2.0 / math.pi)
    inner = coeff * (pre + 0.044715 * pre * pre * pre)
    tangent = jnp.tanh(inner)
    value = 0.5 * pre * (1.0 + tangent)
    deriv = 0.5 * (1.0 + tangent) + 0.5 * pre * (1.0 - tangent * tangent) * coeff * (1.0 + 3.0 * 0.044715 * pre * pre)
    return (value, deriv)

def normalize(paired):
    values = paired.astype(jnp.float32)
    centered = values - lax.optimization_barrier(jnp.mean(values, axis=-1, keepdims=True))
    inverse = lax.rsqrt(lax.optimization_barrier(jnp.mean(centered * centered, axis=-1, keepdims=True)) + 1e-05)
    return (centered * inverse, inverse)

def unit_forward(paired, w_in, w_out, bias):
    nhat, inverse = normalize(paired)
    normed = nhat.astype(jnp.bfloat16)
    pre = lax.dot_general(normed, w_in, (((1,), (1,)), ((), ())), preferred_element_type=jnp.float32) + bias
    value, deriv = gelu_pair(pre)
    hidden = value.astype(jnp.bfloat16)
    branch = jnp.dot(hidden, w_out, preferred_element_type=jnp.float32)
    return (paired.astype(jnp.float32) + branch).astype(jnp.bfloat16)

def unit_backward(paired, grad_y, w_in, w_out, bias):
    nhat, inverse = normalize(paired)
    normed = nhat.astype(jnp.bfloat16)
    pre = lax.dot_general(normed, w_in, (((1,), (1,)), ((), ())), preferred_element_type=jnp.float32) + bias
    value, deriv = gelu_pair(pre)
    hidden = value.astype(jnp.bfloat16)
    grad_out = lax.dot_general(hidden, grad_y, (((0,), (0,)), ((), ())), preferred_element_type=jnp.float32)
    grad_hidden = lax.dot_general(grad_y, w_out, (((1,), (1,)), ((), ())), preferred_element_type=jnp.float32)
    grad_pre = grad_hidden * deriv
    grad_bias = lax.optimization_barrier(jnp.sum(grad_pre, axis=0))
    grad_pre_b = grad_pre.astype(jnp.bfloat16)
    grad_in = lax.dot_general(grad_pre_b, normed, (((0,), (0,)), ((), ())), preferred_element_type=jnp.float32)
    grad_norm = jnp.dot(grad_pre_b, w_in, preferred_element_type=jnp.float32)
    grad_pair = grad_y.astype(jnp.float32) + inverse * (grad_norm - lax.optimization_barrier(jnp.mean(grad_norm, axis=-1, keepdims=True)) - nhat * lax.optimization_barrier(jnp.mean(grad_norm * nhat, axis=-1, keepdims=True)))
    return (grad_pair.astype(jnp.bfloat16), grad_in, grad_out, grad_bias)

def make_pairs(values, shift):
    width = values.shape[1]
    blocks = values.reshape(-1, 2, 2 ** shift, width)
    return jnp.concatenate([blocks[:, 0], blocks[:, 1]], axis=-1).reshape(-1, 2 * width)

def undo_pairs(paired, shift):
    width = paired.shape[1] // 2
    blocks = paired.reshape(-1, 2 ** shift, 2, width)
    return jnp.transpose(blocks, (0, 2, 1, 3)).reshape(-1, width)

def reference(inputs, upstream, w_in, w_out, bias):
    row_bits = bit_count(ROWS)
    lo_bits = bit_count(N_LO)
    hi_bits = bit_count(N_HI)
    shifts = [row_bits + lo_bits + hi_bits - 1, row_bits + lo_bits - 1, row_bits + lo_bits, row_bits]
    current = inputs
    saved = []
    for shift in shifts:
        paired = make_pairs(current, shift)
        saved.append(paired)
        current = undo_pairs(unit_forward(paired, w_in, w_out, bias), shift)
    features_out = current
    grads = upstream
    total_in = jnp.zeros(w_in.shape, jnp.float32)
    total_out = jnp.zeros(w_out.shape, jnp.float32)
    total_bias = jnp.zeros(bias.shape, jnp.float32)
    for section in range(len(shifts) - 1, -1, -1):
        shift = shifts[section]
        grad_y = make_pairs(grads, shift)
        grad_pair, part_in, part_out, part_bias = unit_backward(saved[section], grad_y, w_in, w_out, bias)
        total_in = total_in + part_in
        total_out = total_out + part_out
        total_bias = total_bias + part_bias
        grads = undo_pairs(grad_pair, shift)
    factor = 1.0 / math.sqrt(float(TOKENS))
    return (features_out, grads, total_in * factor, total_out * factor, total_bias * factor)
```

```python
import math

import jax
import jax.numpy as jnp
from jax import lax
from jax.experimental import pallas as pl
from jax.experimental.pallas import tpu as pltpu
from jax.sharding import Mesh
from jax.sharding import PartitionSpec as P

BITS = ("y1", "y0", "zh", "core", "zl1", "zl0", "x1", "x0")
SECTION_GROUP = ("y1", "core", "zl1", "x0")
PLANE_GROUP = ("y1", "y0", "x1", "x0")
COLUMN_GROUP = ("zh", "zl1", "zl0")
HIDDEN, WIDTH, PAIR = 768, 192, 384
QUARTER = 48
CHUNK = 256
BF16, F32 = jnp.bfloat16, jnp.float32
VMEM_LIMIT = 56 * 1024 * 1024


def swap_groups(parts):
    lane = lax.broadcasted_iota(jnp.int32, parts[0].shape, 1)
    for stride, at in ((2, 64), (1, 32)):
        low = (lane & at) == 0
        out = list(parts)
        for i in range(4):
            if not i & stride:
                a, b = parts[i], parts[i | stride]
                out[i] = jnp.where(low, a, pltpu.roll(b, at, 1))
                out[i | stride] = jnp.where(low, pltpu.roll(a, 128 - at, 1), b)
        parts = out
    return parts


def quarters(tile):
    return [tile[QUARTER * q : QUARTER * (q + 1)] for q in range(4)]


def group_of(y1, core, zl1, x0):
    return 8 * y1 + 4 * core + 2 * zl1 + x0


def pack_kernel(x_ref, g_ref, out_ref):
    for at, ref in enumerate((x_ref, g_ref)):
        for t in range(4):
            tile = ref[:, 128 * t : 128 * (t + 1)].astype(F32)
            for g, part in enumerate(swap_groups(quarters(tile))):
                out_ref[4 * t + g, QUARTER * at : QUARTER * (at + 1), :] = part.astype(BF16)


def unpack_kernel(in_ref, f_ref, g_ref):
    for at, ref in enumerate((f_ref, g_ref)):
        for t in range(4):
            parts = [
                in_ref[4 * t + g, QUARTER * at : QUARTER * (at + 1), :].astype(F32) for g in range(4)
            ]
            for q, part in enumerate(swap_groups(parts)):
                ref[QUARTER * q : QUARTER * (q + 1), 128 * t : 128 * (t + 1)] = part.astype(BF16)


def order_kernel(core_ref, w_in_ref, w_out_ref, bias_ref, win_ref, wint_ref, wout_ref, woutt_ref, b_ref):
    core = core_ref[0]

    def place(unit):
        device = (unit * 21846) >> 16
        third = unit - 3 * device
        block = (device >> 6) * 4 + (device & 3)
        z = ((device >> 5) & 1) * 4 + ((device >> 2) & 3)
        return (((device >> 4) & 1) ^ core) * (HIDDEN // 2) + block * 24 + third * 8 + z

    shape = (HIDDEN, HIDDEN)
    hit = lax.broadcasted_iota(jnp.int32, shape, 0) == place(lax.broadcasted_iota(jnp.int32, shape, 1))
    pick = hit.astype(F32).astype(BF16)
    for ref, out, out_t in ((w_in_ref, win_ref, wint_ref), (w_out_ref, wout_ref, woutt_ref)):
        moved = jnp.dot(pick, ref[...], preferred_element_type=F32)
        out[...] = moved.astype(BF16)
        out_t[...] = moved.T.astype(BF16)
    moved = jnp.sum(jnp.where(hit, bias_ref[...], 0.0), axis=1, keepdims=True)
    b_ref[...] = jnp.broadcast_to(moved, (HIDDEN, 128))


def gelu_pair(pre):
    coeff = math.sqrt(2.0 / math.pi)
    square = pre * pre
    tangent = jnp.tanh(coeff * pre * (1.0 + 0.044715 * square))
    half = 0.5 * (1.0 + tangent)
    value = pre * half
    deriv = half + 0.5 * coeff * pre * (1.0 - tangent * tangent) * (1.0 + 3.0 * 0.044715 * square)
    return value, deriv


def pair_tiles(tiles, bit):
    other = 3 - bit
    return jnp.concatenate(
        [
            jnp.concatenate([tiles[0], tiles[other]], axis=1),
            jnp.concatenate([tiles[bit], tiles[3]], axis=1),
        ],
        axis=0,
    )


def unpair_tiles(pairs, bit):
    other = 3 - bit
    tiles = [None] * 4
    tiles[0], tiles[other] = pairs[:WIDTH, :128], pairs[:WIDTH, 128:]
    tiles[bit], tiles[3] = pairs[WIDTH:, :128], pairs[WIDTH:, 128:]
    return tiles


def swap_tiles(tiles):
    split = [quarters(t.astype(F32)) for t in tiles]
    moved = [swap_groups([split[t][q] for t in range(4)]) for q in range(4)]
    return [jnp.concatenate([moved[q][t] for q in range(4)], axis=0).astype(BF16) for t in range(4)]


def main_kernel(
    in_ref, win_ref, wint_ref, wout_ref, woutt_ref, b_ref,
    ret_ref, keep_ref, send_ref,
    n_ref, nhat_ref, inv_ref, h_ref, dv_ref, gp_ref, gy_ref, gb_ref,
):
    def load(at, block):
        tiles = []
        for t in range(4):
            parts = [in_ref[block(t, g), QUARTER * at : QUARTER * (at + 1), :].astype(F32) for g in range(4)]
            tiles.append(jnp.concatenate(swap_groups(parts), axis=0).astype(BF16))
        return tiles

    def store(at, tiles, block):
        for t in range(4):
            for g, part in enumerate(swap_groups(quarters(tiles[t].astype(F32)))):
                ret_ref[block(t, g), QUARTER * at : QUARTER * (at + 1), :] = part.astype(BF16)

    def by_high(t, g):
        return group_of(t >> 1, g >> 1, t & 1, g & 1)

    def by_low(t, g):
        return group_of(g >> 1, t >> 1, g & 1, t & 1)

    bits = (2, 1, 2, 1)
    tiles = load(0, by_high)
    for s in range(4):
        if s == 2:
            tiles = swap_tiles(tiles)
        pairs = pair_tiles(tiles, bits[s])
        values = pairs.astype(F32)
        centered = values - jnp.mean(values, axis=0, keepdims=True)
        inverse = lax.rsqrt(jnp.mean(centered * centered, axis=0, keepdims=True) + 1e-05)
        nhat = centered * inverse
        normed = nhat.astype(BF16)
        n_ref[s] = normed
        nhat_ref[s] = nhat
        inv_ref[s] = jnp.broadcast_to(inverse, (8, CHUNK))
        for j in range(3):
            rows = slice(CHUNK * j, CHUNK * (j + 1))
            bias = b_ref[rows, :]
            pre = jnp.dot(win_ref[rows, :], normed, preferred_element_type=F32)
            pre = pre + jnp.concatenate([bias, bias], axis=1)
            value, deriv = gelu_pair(pre)
            h_ref[s, rows, :] = value.astype(BF16)
            dv_ref[s, rows, :] = deriv
        branch = jnp.dot(woutt_ref[...], h_ref[s], preferred_element_type=F32)
        tiles = unpair_tiles((values + branch).astype(BF16), bits[s])
    store(0, tiles, by_low)

    tiles = load(1, by_low)
    for s in range(3, -1, -1):
        if s == 1:
            tiles = swap_tiles(tiles)
        grad_y = pair_tiles(tiles, bits[s])
        gy_ref[s] = grad_y
        for j in range(3):
            rows = slice(CHUNK * j, CHUNK * (j + 1))
            grad_pre = jnp.dot(wout_ref[rows, :], grad_y, preferred_element_type=F32) * dv_ref[s, rows, :]
            gp_ref[s, rows, :] = grad_pre.astype(BF16)
            folded = grad_pre[:, :128] + grad_pre[:, 128:]
            if s == 3:
                gb_ref[rows, :] = folded
            else:
                gb_ref[rows, :] += folded
        grad_norm = jnp.dot(wint_ref[...], gp_ref[s], preferred_element_type=F32)
        nhat = nhat_ref[s]
        grad_pair = grad_y.astype(F32) + inv_ref[s, 0:1, :] * (
            grad_norm
            - jnp.mean(grad_norm, axis=0, keepdims=True)
            - nhat * jnp.mean(grad_norm * nhat, axis=0, keepdims=True)
        )
        tiles = unpair_tiles(grad_pair.astype(BF16), bits[s])
    store(1, tiles, by_high)

    def over_positions(a, b):
        return lax.dot_general(a, b, (((1,), (1,)), ((), ())), preferred_element_type=F32)

    lane = lax.broadcasted_iota(jnp.int32, (8, PAIR), 1)
    for j in range(4):
        rows = slice(WIDTH * j, WIDTH * (j + 1))
        grad_in = sum(over_positions(gp_ref[s, rows, :], n_ref[s]) for s in range(4))
        grad_out = sum(over_positions(h_ref[s, rows, :], gy_ref[s]) for s in range(4))
        grad_bias = jnp.sum(gb_ref[rows, :], axis=1, keepdims=True)
        for b in range(8):
            at = slice(24 * b, 24 * (b + 1))
            thirds = [grad_bias[24 * b + 8 * k : 24 * b + 8 * (k + 1)] for k in range(3)]
            extra = jnp.where(lane == 0, thirds[0], jnp.where(lane == 1, thirds[1], thirds[2]))
            block = jnp.concatenate([grad_in[at], grad_out[at], extra], axis=0).astype(BF16)
            (keep_ref if j < 2 else send_ref)[8 * (j % 2) + b] = block


def plane_kernel(in_ref, out_ref, total_ref):
    total = in_ref[0].astype(F32)
    for i in range(1, 16):
        total = total + in_ref[i].astype(F32)
    total_ref[0:56, :] = total
    total_ref[56:64, :] = jnp.zeros((8, PAIR), F32)
    for z in range(8):
        out_ref[z] = jnp.concatenate([total_ref[8 * i + z : 8 * i + z + 1, :] for i in range(8)], axis=0)


def call(kernel, out_shapes, scratch=(), smem=0, **args):
    vmem = pl.BlockSpec(memory_space=pltpu.VMEM)
    spec = [pl.BlockSpec(memory_space=pltpu.SMEM)] * smem

    def run(*operands):
        return pl.pallas_call(
            kernel,
            out_shape=out_shapes,
            in_specs=spec + [vmem] * (len(operands) - smem),
            out_specs=jax.tree.map(lambda _: vmem, out_shapes),
            scratch_shapes=scratch,
            compiler_params=pltpu.CompilerParams(vmem_limit_bytes=VMEM_LIMIT),
            **args,
        )(*operands)

    return run


def shape(*dims, dtype=BF16):
    return jax.ShapeDtypeStruct(dims, dtype)


def on_device(inputs, upstream, w_in, w_out, bias):
    rows, width = inputs.shape
    tokens = rows * lax.axis_size(BITS)
    core = lax.axis_index("core").astype(jnp.int32).reshape(1)
    packed = call(pack_kernel, shape(16, 2 * QUARTER, 128))(inputs.T, upstream.T)
    blocks = lax.all_to_all(packed, SECTION_GROUP, 0, 0, tiled=True)
    ordered = call(
        order_kernel,
        (
            shape(HIDDEN, PAIR), shape(PAIR, HIDDEN), shape(HIDDEN, PAIR), shape(PAIR, HIDDEN),
            shape(HIDDEN, 128, dtype=F32),
        ),
        smem=1,
    )(core, w_in, w_out, bias.reshape(1, HIDDEN))
    back, keep, send = call(
        main_kernel,
        (shape(16, 2 * QUARTER, 128), shape(16, 56, PAIR), shape(16, 56, PAIR)),
        scratch=(
            pltpu.VMEM((4, PAIR, CHUNK), BF16),
            pltpu.VMEM((4, PAIR, CHUNK), F32),
            pltpu.VMEM((4, 8, CHUNK), F32),
            pltpu.VMEM((4, HIDDEN, CHUNK), BF16),
            pltpu.VMEM((4, HIDDEN, CHUNK), F32),
            pltpu.VMEM((4, HIDDEN, CHUNK), BF16),
            pltpu.VMEM((4, PAIR, CHUNK), BF16),
            pltpu.VMEM((HIDDEN, 128), F32),
        ),
    )(blocks, *ordered)
    other = lax.ppermute(send, "core", [(0, 1), (1, 0)])
    summed = (keep.astype(F32) + other.astype(F32)).astype(BF16)
    plane = lax.all_to_all(summed, PLANE_GROUP, 0, 0, tiled=True)
    columns = call(plane_kernel, shape(8, 8, PAIR, dtype=F32), scratch=(pltpu.VMEM((64, PAIR), F32),))(plane)
    column = lax.all_to_all(columns, COLUMN_GROUP, 0, 0, tiled=True)
    total = jnp.sum(column, axis=0) * (1.0 / math.sqrt(float(tokens)))
    returned = lax.all_to_all(back, SECTION_GROUP, 0, 0, tiled=True)
    features, grads = call(unpack_kernel, (shape(width, rows), shape(width, rows)))(returned)
    return features.T, grads.T, total[0:3], total[3:6], total[6, 0:3]


def solution(mesh):
    bits = Mesh(mesh.devices.reshape((2,) * len(BITS)), BITS)
    in_specs = (P(BITS, None), P(BITS, None), P(), P(), P())
    out_specs = (P(BITS, None), P(BITS, None), P(BITS, None), P(BITS, None), P(BITS))
    return jax.shard_map(on_device, mesh=bits, in_specs=in_specs, out_specs=out_specs, check_vma=False)
```

```python
import functools
import math

import jax
import jax.numpy as jnp
from jax import lax
from jax.experimental import pallas as pl
from jax.experimental.pallas import tpu as pltpu
from jax.sharding import Mesh
from jax.sharding import PartitionSpec as P

BITS = ("y1", "y0", "zh", "core", "zl1", "zl0", "x1", "x0")
SECTION_GROUP = ("y1", "core", "zl1", "x0")
PLANE_GROUP = ("y1", "y0", "x1", "x0")
COLUMN_GROUP = ("zh", "zl1", "zl0")
HIDDEN, WIDTH, PAIR = 768, 192, 384
OUT_AT = PAIR + 128
WIDE = PAIR + 16
QUARTER = 48
BLOCK = 152
CHUNK = 256
BF16, F32 = jnp.bfloat16, jnp.float32
MIB = 1024 * 1024


def swap_groups(parts):
    lane = lax.broadcasted_iota(jnp.int32, parts[0].shape, 1)
    for stride, at in ((2, 64), (1, 32)):
        low = (lane & at) == 0
        out = list(parts)
        for i in range(4):
            if not i & stride:
                a, b = parts[i], parts[i | stride]
                out[i] = jnp.where(low, a, pltpu.roll(b, at, 1))
                out[i | stride] = jnp.where(low, pltpu.roll(a, 128 - at, 1), b)
        parts = out
    return parts


def quarters(tile):
    return [tile[QUARTER * q : QUARTER * (q + 1)] for q in range(4)]


def group_of(y1, core, zl1, x0):
    return 8 * y1 + 4 * core + 2 * zl1 + x0


def pack_kernel(x_hbm, g_hbm, out_ref, x_ref, g_ref, sems):
    copies = [
        pltpu.make_async_copy(x_hbm, x_ref, sems.at[0]),
        pltpu.make_async_copy(g_hbm, g_ref, sems.at[1]),
    ]
    for copy in copies:
        copy.start()
    for at, ref in enumerate((x_ref, g_ref)):
        copies[at].wait()
        for t in range(4):
            tile = ref[:, 128 * t : 128 * (t + 1)].astype(F32)
            for g, part in enumerate(swap_groups(quarters(tile))):
                out_ref[4 * t + g, QUARTER * at : QUARTER * (at + 1), :] = part.astype(BF16)


def unpack_kernel(me_ref, in_ref, f_ref, g_ref):
    me = me_ref[0]
    for at, ref in enumerate((f_ref, g_ref)):
        for t in range(4):
            parts = [
                in_ref[me ^ (4 * t + g), QUARTER * at : QUARTER * (at + 1), :].astype(F32) for g in range(4)
            ]
            for q, part in enumerate(swap_groups(parts)):
                ref[QUARTER * q : QUARTER * (q + 1), 128 * t : 128 * (t + 1)] = part.astype(BF16)


def order_kernel(core_ref, w_in_ref, w_out_ref, bias_ref, w_ref, wt_ref):
    core = core_ref[0]

    def place(unit):
        device = (unit * 21846) >> 16
        third = unit - 3 * device
        block = (device >> 6) * 4 + (device & 3)
        z = ((device >> 5) & 1) * 4 + ((device >> 2) & 3)
        return (((device >> 4) & 1) ^ core) * (HIDDEN // 2) + block * 24 + third * 8 + z

    shape = (HIDDEN, HIDDEN)
    hit = lax.broadcasted_iota(jnp.int32, shape, 0) == place(lax.broadcasted_iota(jnp.int32, shape, 1))
    pick = hit.astype(F32).astype(BF16)
    for i, (ref, at) in enumerate(((w_in_ref, 0), (w_out_ref, OUT_AT))):
        moved = jnp.dot(pick, ref[...], preferred_element_type=F32)
        w_ref[:, at : at + PAIR] = moved.astype(BF16)
        wt_ref[PAIR * i : PAIR * (i + 1), :] = moved.T.astype(BF16)
    bias = jnp.sum(jnp.where(hit, bias_ref[...], 0.0), axis=1, keepdims=True)
    lane = lax.broadcasted_iota(jnp.int32, (HIDDEN, 128), 1)
    columns = jnp.zeros((HIDDEN, 128), F32)
    for i in range(3):
        piece = bias.astype(BF16).astype(F32)
        columns = jnp.where(lane == i, piece, columns)
        bias = bias - piece
    w_ref[:, PAIR : PAIR + 128] = columns.astype(BF16)


def gelu_pair(pre):
    coeff = math.sqrt(2.0 / math.pi)
    square = pre * pre
    tangent = jnp.tanh(coeff * pre * (1.0 + 0.044715 * square))
    half = 0.5 * (1.0 + tangent)
    value = pre * half
    deriv = half + 0.5 * coeff * pre * (1.0 - tangent * tangent) * (1.0 + 3.0 * 0.044715 * square)
    return value, deriv


def pair_tiles(tiles, bit):
    other = 3 - bit
    return jnp.concatenate(
        [
            jnp.concatenate([tiles[0], tiles[other]], axis=1),
            jnp.concatenate([tiles[bit], tiles[3]], axis=1),
        ],
        axis=0,
    )


def unpair_tiles(pairs, bit):
    other = 3 - bit
    tiles = [None] * 4
    tiles[0], tiles[other] = pairs[:WIDTH, :128], pairs[:WIDTH, 128:]
    tiles[bit], tiles[3] = pairs[WIDTH:, :128], pairs[WIDTH:, 128:]
    return tiles


def swap_tiles(tiles):
    split = [quarters(t.astype(F32)) for t in tiles]
    moved = [swap_groups([split[t][q] for t in range(4)]) for q in range(4)]
    return [jnp.concatenate([moved[q][t] for q in range(4)], axis=0).astype(BF16) for t in range(4)]


def main_kernel(
    me_ref, in_ref, w_ref, wt_ref,
    ret_ref, keep_ref, send_ref,
    n_ref, nhat_ref, inv_ref, h_ref, dv_ref, gp_ref, gy_ref,
):
    me = me_ref[0]

    def load(at, block):
        tiles = []
        for t in range(4):
            parts = [in_ref[block(t, g), QUARTER * at : QUARTER * (at + 1), :].astype(F32) for g in range(4)]
            tiles.append(jnp.concatenate(swap_groups(parts), axis=0).astype(BF16))
        return tiles

    def store(at, tiles, block):
        for t in range(4):
            for g, part in enumerate(swap_groups(quarters(tiles[t].astype(F32)))):
                ret_ref[me ^ block(t, g), QUARTER * at : QUARTER * (at + 1), :] = part.astype(BF16)

    def by_high(t, g):
        return group_of(t >> 1, g >> 1, t & 1, g & 1)

    def by_low(t, g):
        return group_of(g >> 1, t >> 1, g & 1, t & 1)

    bits = (2, 1, 2, 1)
    ones = (lax.broadcasted_iota(jnp.int32, (WIDE - PAIR, CHUNK), 0) < 3).astype(F32)
    tiles = load(0, by_high)
    for s in range(4):
        if s == 2:
            tiles = swap_tiles(tiles)
        pairs = pair_tiles(tiles, bits[s])
        values = pairs.astype(F32)
        centered = values - jnp.mean(values, axis=0, keepdims=True)
        inverse = lax.rsqrt(jnp.mean(centered * centered, axis=0, keepdims=True) + 1e-05)
        nhat = centered * inverse
        normed = jnp.concatenate([nhat, ones], axis=0).astype(BF16)
        n_ref[s] = normed
        nhat_ref[s] = nhat
        inv_ref[s] = jnp.broadcast_to(inverse, (8, CHUNK))
        for j in range(3):
            rows = slice(CHUNK * j, CHUNK * (j + 1))
            pre = jnp.dot(w_ref[rows, :WIDE], normed, preferred_element_type=F32)
            value, deriv = gelu_pair(pre)
            h_ref[s, rows, :] = value.astype(BF16)
            dv_ref[s, rows, :] = deriv
        branch = jnp.dot(wt_ref[PAIR:, :], h_ref[s], preferred_element_type=F32)
        tiles = unpair_tiles((values + branch).astype(BF16), bits[s])
    store(0, tiles, by_low)

    tiles = load(1, by_low)
    for s in range(3, -1, -1):
        if s == 1:
            tiles = swap_tiles(tiles)
        grad_y = pair_tiles(tiles, bits[s])
        gy_ref[s] = grad_y
        for j in range(3):
            rows = slice(CHUNK * j, CHUNK * (j + 1))
            grad_pre = jnp.dot(w_ref[rows, OUT_AT:], grad_y, preferred_element_type=F32) * dv_ref[s, rows, :]
            gp_ref[s, rows, :] = grad_pre.astype(BF16)
        grad_norm = jnp.dot(wt_ref[:PAIR, :], gp_ref[s], preferred_element_type=F32)
        nhat = nhat_ref[s]
        grad_pair = grad_y.astype(F32) + inv_ref[s, 0:1, :] * (
            grad_norm
            - jnp.mean(grad_norm, axis=0, keepdims=True)
            - nhat * jnp.mean(grad_norm * nhat, axis=0, keepdims=True)
        )
        tiles = unpair_tiles(grad_pair.astype(BF16), bits[s])
    store(1, tiles, by_high)

    def over_positions(a, b):
        return lax.dot_general(a, b, (((1,), (1,)), ((), ())), preferred_element_type=F32)

    lane = lax.broadcasted_iota(jnp.int32, (8, 128), 1)
    for j in range(4):
        rows = slice(WIDTH * j, WIDTH * (j + 1))
        grad_in = sum(over_positions(gp_ref[s, rows, :], n_ref[s]) for s in range(4))
        grad_out = sum(over_positions(h_ref[s, rows, :], gy_ref[s]) for s in range(4))
        for b in range(8):
            at = slice(24 * b, 24 * (b + 1))
            tiles = [g[at, 128 * i : 128 * (i + 1)] for g in (grad_in, grad_out) for i in range(3)]
            thirds = [grad_in[24 * b + 8 * k : 24 * b + 8 * (k + 1), PAIR : PAIR + 1] for k in range(3)]
            extra = jnp.where(lane == 0, thirds[0], jnp.where(lane == 1, thirds[1], thirds[2]))
            (keep_ref if j < 2 else send_ref)[8 * (j % 2) + b] = jnp.concatenate(tiles + [extra], axis=0).astype(BF16)


def plane_kernel(in_ref, out_ref, total_ref):
    total = in_ref[0].astype(F32)
    for i in range(1, 16):
        total = total + in_ref[i].astype(F32)
    total_ref[...] = total
    for z in range(8):
        rows = [total_ref[pl.ds(z, 19, stride=8), :], jnp.zeros((5, 128), F32)]
        out_ref[z] = jnp.concatenate(rows, axis=0).astype(BF16)


def column_kernel(factor, in_ref, w_in_ref, w_out_ref, bias_ref):
    total = in_ref[0].astype(F32)
    for i in range(1, 8):
        total = total + in_ref[i].astype(F32)
    total = total * factor
    for i in range(3):
        w_in_ref[:, 128 * i : 128 * (i + 1)] = total[3 * i : 3 * i + 3]
        w_out_ref[:, 128 * i : 128 * (i + 1)] = total[9 + 3 * i : 12 + 3 * i]
    bias_ref[...] = total[18:19, 0:3]


def call(kernel, out_shapes, scratch=(), smem=0, vmem_mib=4, space=None):
    vmem = pl.BlockSpec(memory_space=pltpu.VMEM)
    spec = [pl.BlockSpec(memory_space=pltpu.SMEM)] * smem

    def run(*operands):
        return pl.pallas_call(
            kernel,
            out_shape=out_shapes,
            in_specs=spec + [space or vmem] * (len(operands) - smem),
            out_specs=jax.tree.map(lambda _: vmem, out_shapes),
            scratch_shapes=scratch,
            compiler_params=pltpu.CompilerParams(vmem_limit_bytes=vmem_mib * MIB),
        )(*operands)

    return run


def shape(*dims, dtype=BF16):
    return jax.ShapeDtypeStruct(dims, dtype)


def give_back(blocks):
    held = blocks.reshape((2, 2, 2, 2) + blocks.shape[1:])
    for axis, at in (("core", 1), ("x0", 3), ("zl1", 2), ("y1", 0)):
        stay = lax.index_in_dim(held, 0, at, keepdims=True)
        leave = lax.index_in_dim(held, 1, at, keepdims=True)
        held = jnp.concatenate([stay, swap(leave, axis)], axis=at)
    return held.reshape(blocks.shape)


def swap(block, axis):
    return lax.ppermute(block, axis, [(0, 1), (1, 0)])


def on_device(inputs, upstream, w_in, w_out, bias):
    rows, width = inputs.shape
    tokens = rows * lax.axis_size(BITS)
    core = lax.axis_index("core").astype(jnp.int32).reshape(1)
    me = sum(lax.axis_index(a).astype(jnp.int32) << (3 - i) for i, a in enumerate(SECTION_GROUP)).reshape(1)
    hbm = pl.BlockSpec(memory_space=pltpu.HBM)
    landing = pltpu.VMEM((width, rows), BF16)
    packed = call(
        pack_kernel, shape(16, 2 * QUARTER, 128), scratch=(landing, landing, pltpu.SemaphoreType.DMA((2,))), space=hbm, vmem_mib=60
    )(inputs.T, upstream.T)
    blocks = lax.all_to_all(packed, SECTION_GROUP, 0, 0, tiled=True)
    ordered = call(order_kernel, (shape(HIDDEN, OUT_AT + PAIR), shape(2 * PAIR, HIDDEN)), smem=1, vmem_mib=12)(
        core, w_in, w_out, bias.reshape(1, HIDDEN)
    )
    back, keep, send = call(
        main_kernel,
        (shape(16, 2 * QUARTER, 128), shape(16, BLOCK, 128), shape(16, BLOCK, 128)),
        scratch=(
            pltpu.VMEM((4, WIDE, CHUNK), BF16),
            pltpu.VMEM((4, PAIR, CHUNK), F32),
            pltpu.VMEM((4, 8, CHUNK), F32),
            pltpu.VMEM((4, HIDDEN, CHUNK), BF16),
            pltpu.VMEM((4, HIDDEN, CHUNK), F32),
            pltpu.VMEM((4, HIDDEN, CHUNK), BF16),
            pltpu.VMEM((4, PAIR, CHUNK), BF16),
        ),
        smem=1,
        vmem_mib=24,
    )(me, blocks, *ordered)
    other = swap(send, "core")
    summed = (keep.astype(F32) + other.astype(F32)).astype(BF16)
    plane = lax.all_to_all(summed, PLANE_GROUP, 0, 0, tiled=True)
    columns = call(plane_kernel, shape(8, 24, 128), scratch=(pltpu.VMEM((BLOCK, 128), F32),))(plane)
    column = lax.all_to_all(columns, COLUMN_GROUP, 0, 0, tiled=True)
    share_in, share_out, share_bias = call(
        functools.partial(column_kernel, 1.0 / math.sqrt(float(tokens))),
        (shape(3, PAIR, dtype=F32), shape(3, PAIR, dtype=F32), shape(1, 3, dtype=F32)),
    )(column)
    features, grads = call(unpack_kernel, (shape(width, rows), shape(width, rows)), smem=1)(me, give_back(back))
    return features.T, grads.T, share_in, share_out, share_bias.reshape(3)


def solution(mesh):
    bits = Mesh(mesh.devices.reshape((2,) * len(BITS)), BITS)
    in_specs = (P(BITS, None), P(BITS, None), P(), P(), P())
    out_specs = (P(BITS, None), P(BITS, None), P(BITS, None), P(BITS, None), P(BITS))
    return jax.shard_map(on_device, mesh=bits, in_specs=in_specs, out_specs=out_specs, check_vma=False)
```

```python
import functools
import math

import jax
import jax.numpy as jnp
from jax import lax
from jax.experimental import pallas as pl
from jax.experimental.pallas import tpu as pltpu
from jax.sharding import Mesh
from jax.sharding import PartitionSpec as P

BITS = ("y1", "y0", "zh", "core", "zl1", "zl0", "x1", "x0")
SECTION_GROUP = ("y1", "core", "zl1", "x0")
PLANE_GROUP = ("y1", "y0", "x1", "x0")
COLUMN_GROUP = ("zh", "zl1", "zl0")
HIDDEN, WIDTH, PAIR = 768, 192, 384
OUT_AT = PAIR + 128
WIDE = PAIR + 16
QUARTER = 48
BLOCK = 152
CHUNK = 256
BF16, F32 = jnp.bfloat16, jnp.float32
MIB = 1024 * 1024


def swap_groups(parts):
    lane = lax.broadcasted_iota(jnp.int32, parts[0].shape, 1)
    for stride, at in ((2, 64), (1, 32)):
        low = (lane & at) == 0
        out = list(parts)
        for i in range(4):
            if not i & stride:
                a, b = parts[i], parts[i | stride]
                out[i] = jnp.where(low, a, pltpu.roll(b, at, 1))
                out[i | stride] = jnp.where(low, pltpu.roll(a, 128 - at, 1), b)
        parts = out
    return parts


def quarters(tile):
    return [tile[QUARTER * q : QUARTER * (q + 1)] for q in range(4)]


def group_of(y1, core, zl1, x0):
    return 8 * y1 + 4 * core + 2 * zl1 + x0


def pack_kernel(x_hbm, g_hbm, out_hbm, in_ref, out_ref, in_sems, out_sems):
    def arrive(at):
        return pltpu.make_async_copy((x_hbm, g_hbm)[at], in_ref.at[at], in_sems.at[at])

    def leave(at):
        place = (slice(None), pl.ds(QUARTER * at, QUARTER))
        return pltpu.make_async_copy(out_ref.at[place], out_hbm.at[place], out_sems.at[at])

    arrive(0).start()
    arrive(1).start()
    for at in range(2):
        arrive(at).wait()
        for t in range(4):
            tile = in_ref[at, :, 128 * t : 128 * (t + 1)].astype(F32)
            for g, part in enumerate(swap_groups(quarters(tile))):
                out_ref[4 * t + g, QUARTER * at : QUARTER * (at + 1), :] = part.astype(BF16)
        leave(at).start()
    leave(0).wait()
    leave(1).wait()


def unpack_kernel(me_ref, in_ref, f_ref, g_ref):
    me = me_ref[0]
    for at, ref in enumerate((f_ref, g_ref)):
        for t in range(4):
            parts = [
                in_ref[me ^ (4 * t + g), QUARTER * at : QUARTER * (at + 1), :].astype(F32) for g in range(4)
            ]
            for q, part in enumerate(swap_groups(parts)):
                ref[QUARTER * q : QUARTER * (q + 1), 128 * t : 128 * (t + 1)] = part.astype(BF16)


def order_kernel(core_ref, w_in_ref, w_out_ref, bias_ref, w_ref, wt_ref):
    core = core_ref[0]

    def place(unit):
        device = (unit * 21846) >> 16
        third = unit - 3 * device
        block = (device >> 6) * 4 + (device & 3)
        z = ((device >> 5) & 1) * 4 + ((device >> 2) & 3)
        return (((device >> 4) & 1) ^ core) * (HIDDEN // 2) + block * 24 + third * 8 + z

    shape = (HIDDEN, HIDDEN)
    hit = lax.broadcasted_iota(jnp.int32, shape, 0) == place(lax.broadcasted_iota(jnp.int32, shape, 1))
    pick = hit.astype(F32).astype(BF16)
    for i, (ref, at) in enumerate(((w_in_ref, 0), (w_out_ref, OUT_AT))):
        moved = jnp.dot(pick, ref[...], preferred_element_type=F32)
        w_ref[:, at : at + PAIR] = moved.astype(BF16)
        wt_ref[PAIR * i : PAIR * (i + 1), :] = moved.T.astype(BF16)
    bias = jnp.sum(jnp.where(hit, bias_ref[...], 0.0), axis=1, keepdims=True)
    lane = lax.broadcasted_iota(jnp.int32, (HIDDEN, 128), 1)
    columns = jnp.zeros((HIDDEN, 128), F32)
    for i in range(3):
        piece = bias.astype(BF16).astype(F32)
        columns = jnp.where(lane == i, piece, columns)
        bias = bias - piece
    w_ref[:, PAIR : PAIR + 128] = columns.astype(BF16)


def gelu_pair(pre):
    coeff = math.sqrt(2.0 / math.pi)
    square = pre * pre
    tangent = jnp.tanh(coeff * pre * (1.0 + 0.044715 * square))
    half = 0.5 * (1.0 + tangent)
    value = pre * half
    deriv = half + 0.5 * coeff * pre * (1.0 - tangent * tangent) * (1.0 + 3.0 * 0.044715 * square)
    return value, deriv


def pair_tiles(tiles, bit):
    other = 3 - bit
    return jnp.concatenate(
        [
            jnp.concatenate([tiles[0], tiles[other]], axis=1),
            jnp.concatenate([tiles[bit], tiles[3]], axis=1),
        ],
        axis=0,
    )


def unpair_tiles(pairs, bit):
    other = 3 - bit
    tiles = [None] * 4
    tiles[0], tiles[other] = pairs[:WIDTH, :128], pairs[:WIDTH, 128:]
    tiles[bit], tiles[3] = pairs[WIDTH:, :128], pairs[WIDTH:, 128:]
    return tiles


def swap_tiles(tiles):
    split = [quarters(t.astype(F32)) for t in tiles]
    moved = [swap_groups([split[t][q] for t in range(4)]) for q in range(4)]
    return [jnp.concatenate([moved[q][t] for q in range(4)], axis=0).astype(BF16) for t in range(4)]


def mdot(a, b):
    n=2
    m=a.shape[0]//n
    return jnp.concatenate([jnp.dot(a[i*m:(i+1)*m], b, preferred_element_type=F32) for i in range(n)],axis=0)


def main_kernel(
    me_ref, in_ref, w_ref, wt_ref,
    ret_ref, keep_ref, send_ref,
    nt_ref, nhat_ref, inv_ref, h_ref, dv_ref, gp_ref, gyt_ref,
):
    me = me_ref[0]

    def load(at, block):
        tiles = []
        for t in range(4):
            parts = [in_ref[block(t, g), QUARTER * at : QUARTER * (at + 1), :].astype(F32) for g in range(4)]
            tiles.append(jnp.concatenate(swap_groups(parts), axis=0).astype(BF16))
        return tiles

    def store(at, tiles, block):
        for t in range(4):
            for g, part in enumerate(swap_groups(quarters(tiles[t].astype(F32)))):
                ret_ref[me ^ block(t, g), QUARTER * at : QUARTER * (at + 1), :] = part.astype(BF16)

    def by_high(t, g):
        return group_of(t >> 1, g >> 1, t & 1, g & 1)

    def by_low(t, g):
        return group_of(g >> 1, t >> 1, g & 1, t & 1)

    bits = (2, 1, 2, 1)
    ones = (lax.broadcasted_iota(jnp.int32, (WIDE - PAIR, CHUNK), 0) < 3).astype(F32)
    tiles = load(0, by_high)
    for s in range(4):
        if s == 2:
            tiles = swap_tiles(tiles)
        pairs = pair_tiles(tiles, bits[s])
        values = pairs.astype(F32)
        centered = values - jnp.mean(values, axis=0, keepdims=True)
        inverse = lax.rsqrt(jnp.mean(centered * centered, axis=0, keepdims=True) + 1e-05)
        nhat = centered * inverse
        normed = jnp.concatenate([nhat, ones], axis=0).astype(BF16)
        nt_ref[CHUNK * s : CHUNK * (s + 1), :] = normed.T
        nhat_ref[s] = nhat
        inv_ref[s] = jnp.broadcast_to(inverse, (8, CHUNK))
        for j in range(6):
            rows = slice(128 * j, 128 * (j + 1))
            pre = jnp.dot(w_ref[rows, :WIDE], normed, preferred_element_type=F32)
            value, deriv = gelu_pair(pre)
            h_ref[rows, CHUNK * s : CHUNK * (s + 1)] = value.astype(BF16)
            dv_ref[s, rows, :] = deriv
        branch = mdot(wt_ref[PAIR:, :], h_ref[:, CHUNK * s : CHUNK * (s + 1)])
        tiles = unpair_tiles((values + branch).astype(BF16), bits[s])
    store(0, tiles, by_low)

    tiles = load(1, by_low)
    for s in range(3, -1, -1):
        if s == 1:
            tiles = swap_tiles(tiles)
        grad_y = pair_tiles(tiles, bits[s])
        gyt_ref[CHUNK * s : CHUNK * (s + 1), :] = grad_y.T
        for j in range(6):
            rows = slice(128 * j, 128 * (j + 1))
            grad_pre = jnp.dot(w_ref[rows, OUT_AT:], grad_y, preferred_element_type=F32) * dv_ref[s, rows, :]
            gp_ref[rows, CHUNK * s : CHUNK * (s + 1)] = grad_pre.astype(BF16)
        grad_norm = mdot(wt_ref[:PAIR, :], gp_ref[:, CHUNK * s : CHUNK * (s + 1)])
        nhat = nhat_ref[s]
        grad_pair = grad_y.astype(F32) + inv_ref[s, 0:1, :] * (
            grad_norm
            - jnp.mean(grad_norm, axis=0, keepdims=True)
            - nhat * jnp.mean(grad_norm * nhat, axis=0, keepdims=True)
        )
        tiles = unpair_tiles(grad_pair.astype(BF16), bits[s])
    store(1, tiles, by_high)

    lane = lax.broadcasted_iota(jnp.int32, (8, 128), 1)
    for j in range(2):
        rows = slice(PAIR * j, PAIR * (j + 1))
        grad_in = jnp.dot(gp_ref[rows, :], nt_ref[...], preferred_element_type=F32)
        grad_out = jnp.dot(h_ref[rows, :], gyt_ref[...], preferred_element_type=F32)
        for b in range(16):
            at = slice(24 * b, 24 * (b + 1))
            tiles = [g[at, 128 * i : 128 * (i + 1)] for g in (grad_in, grad_out) for i in range(3)]
            thirds = [grad_in[24 * b + 8 * k : 24 * b + 8 * (k + 1), PAIR : PAIR + 1] for k in range(3)]
            extra = jnp.where(lane == 0, thirds[0], jnp.where(lane == 1, thirds[1], thirds[2]))
            (send_ref if j else keep_ref)[b] = jnp.concatenate(tiles + [extra], axis=0).astype(BF16)


def plane_kernel(in_ref, out_ref, total_ref):
    total = in_ref[0].astype(F32)
    for i in range(1, 16):
        total = total + in_ref[i].astype(F32)
    total_ref[...] = total
    for z in range(8):
        rows = [total_ref[pl.ds(z, 19, stride=8), :], jnp.zeros((5, 128), F32)]
        out_ref[z] = jnp.concatenate(rows, axis=0).astype(BF16)


def column_kernel(factor, in_ref, w_in_ref, w_out_ref, bias_ref):
    total = in_ref[0].astype(F32)
    for i in range(1, 8):
        total = total + in_ref[i].astype(F32)
    total = total * factor
    for i in range(3):
        w_in_ref[:, 128 * i : 128 * (i + 1)] = total[3 * i : 3 * i + 3]
        w_out_ref[:, 128 * i : 128 * (i + 1)] = total[9 + 3 * i : 12 + 3 * i]
    bias_ref[...] = total[18:19, 0:3]


def call(kernel, out_shapes, scratch=(), smem=0, vmem_mib=4, space=None):
    vmem = pl.BlockSpec(memory_space=pltpu.VMEM)
    spec = [pl.BlockSpec(memory_space=pltpu.SMEM)] * smem

    def run(*operands):
        return pl.pallas_call(
            kernel,
            out_shape=out_shapes,
            in_specs=spec + [space or vmem] * (len(operands) - smem),
            out_specs=jax.tree.map(lambda _: space or vmem, out_shapes),
            scratch_shapes=scratch,
            compiler_params=pltpu.CompilerParams(vmem_limit_bytes=vmem_mib * MIB),
        )(*operands)

    return run


def shape(*dims, dtype=BF16):
    return jax.ShapeDtypeStruct(dims, dtype)


def run_main(me, blocks, weights, turned):
    return call(
        main_kernel,
        (shape(16, 2 * QUARTER, 128), shape(16, BLOCK, 128), shape(16, BLOCK, 128)),
        scratch=(
            pltpu.VMEM((4 * CHUNK, WIDE), BF16),
            pltpu.VMEM((4, PAIR, CHUNK), F32),
            pltpu.VMEM((4, 8, CHUNK), F32),
            pltpu.VMEM((HIDDEN, 4 * CHUNK), BF16),
            pltpu.VMEM((4, HIDDEN, CHUNK), F32),
            pltpu.VMEM((HIDDEN, 4 * CHUNK), BF16),
            pltpu.VMEM((4 * CHUNK, PAIR), BF16),
        ),
        smem=1,
        vmem_mib=24,
    )(me, blocks, weights, turned)


def give_back(blocks):
    held = blocks.reshape((2, 2, 2, 2) + blocks.shape[1:])
    for axis, at in (("core", 1), ("x0", 3), ("zl1", 2), ("y1", 0)):
        stay = lax.index_in_dim(held, 0, at, keepdims=True)
        leave = lax.index_in_dim(held, 1, at, keepdims=True)
        held = jnp.concatenate([stay, swap(leave, axis)], axis=at)
    return held.reshape(blocks.shape)


def swap(block, axis):
    return lax.ppermute(block, axis, [(0, 1), (1, 0)])


def on_device(inputs, upstream, w_in, w_out, bias):
    rows, width = inputs.shape
    tokens = rows * lax.axis_size(BITS)
    core = lax.axis_index("core").astype(jnp.int32).reshape(1)
    me = sum(lax.axis_index(a).astype(jnp.int32) << (3 - i) for i, a in enumerate(SECTION_GROUP)).reshape(1)
    packed = call(
        pack_kernel,
        shape(16, 2 * QUARTER, 128),
        scratch=(
            pltpu.VMEM((2, width, rows), BF16),
            pltpu.VMEM((16, 2 * QUARTER, 128), BF16),
            pltpu.SemaphoreType.DMA((2,)),
            pltpu.SemaphoreType.DMA((2,)),
        ),
        space=pl.BlockSpec(memory_space=pltpu.HBM),
        vmem_mib=60,
    )(inputs.T, upstream.T)
    blocks = lax.all_to_all(packed, SECTION_GROUP, 0, 0, tiled=True)
    ordered = call(order_kernel, (shape(HIDDEN, OUT_AT + PAIR), shape(2 * PAIR, HIDDEN)), smem=1, vmem_mib=12)(
        core, w_in, w_out, bias.reshape(1, HIDDEN)
    )
    back, keep, send = run_main(me, blocks, *ordered)
    other = swap(send, "core")
    summed = (keep.astype(F32) + other.astype(F32)).astype(BF16)
    plane = lax.all_to_all(summed, PLANE_GROUP, 0, 0, tiled=True)
    columns = call(plane_kernel, shape(8, 24, 128), scratch=(pltpu.VMEM((BLOCK, 128), F32),))(plane)
    column = lax.all_to_all(columns, COLUMN_GROUP, 0, 0, tiled=True)
    share_in, share_out, share_bias = call(
        functools.partial(column_kernel, 1.0 / math.sqrt(float(tokens))),
        (shape(3, PAIR, dtype=F32), shape(3, PAIR, dtype=F32), shape(1, 3, dtype=F32)),
    )(column)
    features, grads = call(unpack_kernel, (shape(width, rows), shape(width, rows)), smem=1)(me, give_back(back))
    return features.T, grads.T, share_in, share_out, share_bias.reshape(3)


def solution(mesh):
    bits = Mesh(mesh.devices.reshape((2,) * len(BITS)), BITS)
    in_specs = (P(BITS, None), P(BITS, None), P(), P(), P())
    out_specs = (P(BITS, None), P(BITS, None), P(BITS, None), P(BITS, None), P(BITS))
    return jax.shard_map(on_device, mesh=bits, in_specs=in_specs, out_specs=out_specs, check_vma=False)
```

```python
import functools
import math

import jax
import jax.numpy as jnp
from jax import lax
from jax.experimental import pallas as pl
from jax.experimental.pallas import tpu as pltpu
from jax.sharding import Mesh
from jax.sharding import PartitionSpec as P

BITS = ("y1", "y0", "zh", "core", "zl1", "zl0", "x1", "x0")
SECTION_GROUP = ("y1", "core", "zl1", "x0")
PLANE_GROUP = ("y1", "y0", "x1", "x0")
COLUMN_GROUP = ("zh", "zl1", "zl0")
HIDDEN, WIDTH, PAIR = 768, 192, 384
OUT_AT = PAIR + 128
WIDE = PAIR + 16
QUARTER = 48
BLOCK = 152
CHUNK = 256
BF16, F32 = jnp.bfloat16, jnp.float32
MIB = 1024 * 1024


def swap_groups(parts):
    lane = lax.broadcasted_iota(jnp.int32, parts[0].shape, 1)
    for stride, at in ((2, 64), (1, 32)):
        low = (lane & at) == 0
        out = list(parts)
        for i in range(4):
            if not i & stride:
                a, b = parts[i], parts[i | stride]
                if at == 64:
                    crossed = pltpu.roll(jnp.where(low, b, a), at, 1)
                    out[i], out[i | stride] = jnp.where(low, a, crossed), jnp.where(low, crossed, b)
                else:
                    out[i] = jnp.where(low, a, pltpu.roll(b, at, 1))
                    out[i | stride] = jnp.where(low, pltpu.roll(a, 128 - at, 1), b)
        parts = out
    return parts


def quarters(tile):
    return [tile[QUARTER * q : QUARTER * (q + 1)] for q in range(4)]


def group_of(y1, core, zl1, x0):
    return 8 * y1 + 4 * core + 2 * zl1 + x0


def pack_kernel(x_hbm, g_hbm, out_hbm, in_ref, out_ref, in_sems, out_sems):
    def arrive(at):
        return pltpu.make_async_copy((x_hbm, g_hbm)[at], in_ref.at[at], in_sems.at[at])

    def leave(at):
        place = (slice(None), pl.ds(QUARTER * at, QUARTER))
        return pltpu.make_async_copy(out_ref.at[place], out_hbm.at[place], out_sems.at[at])

    arrive(0).start()
    arrive(1).start()
    for at in range(2):
        arrive(at).wait()
        for t in range(4):
            tile = in_ref[at, :, 128 * t : 128 * (t + 1)].astype(F32)
            for g, part in enumerate(swap_groups(quarters(tile))):
                out_ref[4 * t + g, QUARTER * at : QUARTER * (at + 1), :] = part.astype(BF16)
        leave(at).start()
    leave(0).wait()
    leave(1).wait()


def unpack_kernel(me_ref, in_ref, f_ref, g_ref):
    me = me_ref[0]
    for at, ref in enumerate((f_ref, g_ref)):
        for t in range(4):
            parts = [
                in_ref[me ^ (4 * t + g), QUARTER * at : QUARTER * (at + 1), :].astype(F32) for g in range(4)
            ]
            for q, part in enumerate(swap_groups(parts)):
                ref[QUARTER * q : QUARTER * (q + 1), 128 * t : 128 * (t + 1)] = part.astype(BF16)


def order_kernel(core_ref, w_in_ref, w_out_ref, bias_ref, w_ref, wt_ref):
    core = core_ref[0]

    def place(unit):
        device = (unit * 21846) >> 16
        third = unit - 3 * device
        block = (device >> 6) * 4 + (device & 3)
        z = ((device >> 5) & 1) * 4 + ((device >> 2) & 3)
        return (((device >> 4) & 1) ^ core) * (HIDDEN // 2) + block * 24 + third * 8 + z

    shape = (HIDDEN, HIDDEN)
    hit = lax.broadcasted_iota(jnp.int32, shape, 0) == place(lax.broadcasted_iota(jnp.int32, shape, 1))
    pick = hit.astype(F32).astype(BF16)
    for i, (ref, at) in enumerate(((w_in_ref, 0), (w_out_ref, OUT_AT))):
        moved = jnp.dot(pick, ref[...], preferred_element_type=F32)
        w_ref[:, at : at + PAIR] = moved.astype(BF16)
        wt_ref[PAIR * i : PAIR * (i + 1), :] = moved.T.astype(BF16)
    bias = jnp.sum(jnp.where(hit, bias_ref[...], 0.0), axis=1, keepdims=True)
    lane = lax.broadcasted_iota(jnp.int32, (HIDDEN, 128), 1)
    columns = jnp.zeros((HIDDEN, 128), F32)
    for i in range(3):
        piece = bias.astype(BF16).astype(F32)
        columns = jnp.where(lane == i, piece, columns)
        bias = bias - piece
    w_ref[:, PAIR : PAIR + 128] = columns.astype(BF16)


def gelu_pair(pre):
    coeff = math.sqrt(2.0 / math.pi)
    square = pre * pre
    tangent = jnp.tanh(coeff * pre * (1.0 + 0.044715 * square))
    half = 0.5 * (1.0 + tangent)
    value = pre * half
    deriv = half + 0.5 * coeff * pre * (1.0 - tangent * tangent) * (1.0 + 3.0 * 0.044715 * square)
    return value, deriv


def pair_tiles(tiles, bit):
    other = 3 - bit
    return jnp.concatenate(
        [
            jnp.concatenate([tiles[0], tiles[other]], axis=1),
            jnp.concatenate([tiles[bit], tiles[3]], axis=1),
        ],
        axis=0,
    )


def unpair_tiles(pairs, bit):
    other = 3 - bit
    tiles = [None] * 4
    tiles[0], tiles[other] = pairs[:WIDTH, :128], pairs[:WIDTH, 128:]
    tiles[bit], tiles[3] = pairs[WIDTH:, :128], pairs[WIDTH:, 128:]
    return tiles


def swap_tiles(tiles):
    split = [quarters(t.astype(F32)) for t in tiles]
    moved = [swap_groups([split[t][q] for t in range(4)]) for q in range(4)]
    return [jnp.concatenate([moved[q][t] for q in range(4)], axis=0).astype(BF16) for t in range(4)]


def mdot(a, b):
    n=2
    m=a.shape[0]//n
    return jnp.concatenate([jnp.dot(a[i*m:(i+1)*m], b, preferred_element_type=F32) for i in range(n)],axis=0)


def main_kernel(
    me_ref, in_ref, w_ref, wt_ref,
    ret_ref, keep_ref, send_ref,
    nt_ref, nhat_ref, inv_ref, h_ref, dv_ref, gp_ref, gyt_ref,
):
    me = me_ref[0]

    def load(at, block):
        tiles = []
        for t in range(4):
            parts = [in_ref[block(t, g), QUARTER * at : QUARTER * (at + 1), :].astype(F32) for g in range(4)]
            tiles.append(jnp.concatenate(swap_groups(parts), axis=0).astype(BF16))
        return tiles

    def store(at, tiles, block):
        for t in range(4):
            for g, part in enumerate(swap_groups(quarters(tiles[t].astype(F32)))):
                ret_ref[me ^ block(t, g), QUARTER * at : QUARTER * (at + 1), :] = part.astype(BF16)

    def by_high(t, g):
        return group_of(t >> 1, g >> 1, t & 1, g & 1)

    def by_low(t, g):
        return group_of(g >> 1, t >> 1, g & 1, t & 1)

    bits = (2, 1, 2, 1)
    ones = (lax.broadcasted_iota(jnp.int32, (WIDE - PAIR, CHUNK), 0) < 3).astype(F32)
    tiles = load(0, by_high)
    for s in range(4):
        if s == 2:
            tiles = swap_tiles(tiles)
        pairs = pair_tiles(tiles, bits[s])
        values = pairs.astype(F32)
        centered = values - jnp.mean(values, axis=0, keepdims=True)
        inverse = lax.rsqrt(jnp.mean(centered * centered, axis=0, keepdims=True) + 1e-05)
        nhat = centered * inverse
        normed = jnp.concatenate([nhat, ones], axis=0).astype(BF16)
        nt_ref[CHUNK * s : CHUNK * (s + 1), :] = normed.T
        nhat_ref[s] = nhat
        inv_ref[s] = jnp.broadcast_to(inverse, (8, CHUNK))
        for j in range(6):
            rows = slice(128 * j, 128 * (j + 1))
            pre = jnp.dot(w_ref[rows, :WIDE], normed, preferred_element_type=F32)
            value, deriv = gelu_pair(pre)
            h_ref[rows, CHUNK * s : CHUNK * (s + 1)] = value.astype(BF16)
            dv_ref[s, rows, :] = deriv
        branch = mdot(wt_ref[PAIR:, :], h_ref[:, CHUNK * s : CHUNK * (s + 1)])
        tiles = unpair_tiles((values + branch).astype(BF16), bits[s])
    store(0, tiles, by_low)

    tiles = load(1, by_low)
    for s in range(3, -1, -1):
        if s == 1:
            tiles = swap_tiles(tiles)
        grad_y = pair_tiles(tiles, bits[s])
        gyt_ref[CHUNK * s : CHUNK * (s + 1), :] = grad_y.T
        for j in range(6):
            rows = slice(128 * j, 128 * (j + 1))
            grad_pre = jnp.dot(w_ref[rows, OUT_AT:], grad_y, preferred_element_type=F32) * dv_ref[s, rows, :]
            gp_ref[rows, CHUNK * s : CHUNK * (s + 1)] = grad_pre.astype(BF16)
        grad_norm = mdot(wt_ref[:PAIR, :], gp_ref[:, CHUNK * s : CHUNK * (s + 1)])
        nhat = nhat_ref[s]
        grad_pair = grad_y.astype(F32) + inv_ref[s, 0:1, :] * (
            grad_norm
            - jnp.mean(grad_norm, axis=0, keepdims=True)
            - nhat * jnp.mean(grad_norm * nhat, axis=0, keepdims=True)
        )
        tiles = unpair_tiles(grad_pair.astype(BF16), bits[s])
    store(1, tiles, by_high)

    lane = lax.broadcasted_iota(jnp.int32, (8, 128), 1)
    for j in range(2):
        rows = slice(PAIR * j, PAIR * (j + 1))
        grad_in = jnp.dot(gp_ref[rows, :], nt_ref[...], preferred_element_type=F32)
        grad_out = jnp.dot(h_ref[rows, :], gyt_ref[...], preferred_element_type=F32)
        for b in range(16):
            at = slice(24 * b, 24 * (b + 1))
            tiles = [g[at, 128 * i : 128 * (i + 1)] for g in (grad_in, grad_out) for i in range(3)]
            thirds = [grad_in[24 * b + 8 * k : 24 * b + 8 * (k + 1), PAIR : PAIR + 1] for k in range(3)]
            extra = jnp.where(lane == 0, thirds[0], jnp.where(lane == 1, thirds[1], thirds[2]))
            (send_ref if j else keep_ref)[b] = jnp.concatenate(tiles + [extra], axis=0).astype(BF16)


def plane_kernel(in_ref, out_ref, total_ref):
    total = in_ref[0].astype(F32)
    for i in range(1, 16):
        total = total + in_ref[i].astype(F32)
    total_ref[...] = total
    for z in range(8):
        rows = [total_ref[pl.ds(z, 19, stride=8), :], jnp.zeros((5, 128), F32)]
        out_ref[z] = jnp.concatenate(rows, axis=0).astype(BF16)


def column_kernel(factor, in_ref, w_in_ref, w_out_ref, bias_ref):
    total = in_ref[0].astype(F32)
    for i in range(1, 8):
        total = total + in_ref[i].astype(F32)
    total = total * factor
    for i in range(3):
        w_in_ref[:, 128 * i : 128 * (i + 1)] = total[3 * i : 3 * i + 3]
        w_out_ref[:, 128 * i : 128 * (i + 1)] = total[9 + 3 * i : 12 + 3 * i]
    bias_ref[...] = total[18:19, 0:3]


def call(kernel, out_shapes, scratch=(), smem=0, vmem_mib=4, space=None):
    vmem = pl.BlockSpec(memory_space=pltpu.VMEM)
    spec = [pl.BlockSpec(memory_space=pltpu.SMEM)] * smem

    def run(*operands):
        return pl.pallas_call(
            kernel,
            out_shape=out_shapes,
            in_specs=spec + [space or vmem] * (len(operands) - smem),
            out_specs=jax.tree.map(lambda _: space or vmem, out_shapes),
            scratch_shapes=scratch,
            compiler_params=pltpu.CompilerParams(vmem_limit_bytes=vmem_mib * MIB),
        )(*operands)

    return run


def shape(*dims, dtype=BF16):
    return jax.ShapeDtypeStruct(dims, dtype)


def run_main(me, blocks, weights, turned):
    return call(
        main_kernel,
        (shape(16, 2 * QUARTER, 128), shape(16, BLOCK, 128), shape(16, BLOCK, 128)),
        scratch=(
            pltpu.VMEM((4 * CHUNK, WIDE), BF16),
            pltpu.VMEM((4, PAIR, CHUNK), F32),
            pltpu.VMEM((4, 8, CHUNK), F32),
            pltpu.VMEM((HIDDEN, 4 * CHUNK), BF16),
            pltpu.VMEM((4, HIDDEN, CHUNK), F32),
            pltpu.VMEM((HIDDEN, 4 * CHUNK), BF16),
            pltpu.VMEM((4 * CHUNK, PAIR), BF16),
        ),
        smem=1,
        vmem_mib=24,
    )(me, blocks, weights, turned)


def give_back(blocks):
    held = blocks.reshape((2, 2, 2, 2) + blocks.shape[1:])
    for axis, at in (("core", 1), ("x0", 3), ("zl1", 2), ("y1", 0)):
        stay = lax.index_in_dim(held, 0, at, keepdims=True)
        leave = lax.index_in_dim(held, 1, at, keepdims=True)
        held = jnp.concatenate([stay, swap(leave, axis)], axis=at)
    return held.reshape(blocks.shape)


def swap(block, axis):
    return lax.ppermute(block, axis, [(0, 1), (1, 0)])


def on_device(inputs, upstream, w_in, w_out, bias):
    rows, width = inputs.shape
    tokens = rows * lax.axis_size(BITS)
    core = lax.axis_index("core").astype(jnp.int32).reshape(1)
    me = sum(lax.axis_index(a).astype(jnp.int32) << (3 - i) for i, a in enumerate(SECTION_GROUP)).reshape(1)
    packed = call(
        pack_kernel,
        shape(16, 2 * QUARTER, 128),
        scratch=(
            pltpu.VMEM((2, width, rows), BF16),
            pltpu.VMEM((16, 2 * QUARTER, 128), BF16),
            pltpu.SemaphoreType.DMA((2,)),
            pltpu.SemaphoreType.DMA((2,)),
        ),
        space=pl.BlockSpec(memory_space=pltpu.HBM),
        vmem_mib=60,
    )(inputs.T, upstream.T)
    blocks = lax.all_to_all(packed, SECTION_GROUP, 0, 0, tiled=True)
    ordered = call(order_kernel, (shape(HIDDEN, OUT_AT + PAIR), shape(2 * PAIR, HIDDEN)), smem=1, vmem_mib=12)(
        core, w_in, w_out, bias.reshape(1, HIDDEN)
    )
    back, keep, send = run_main(me, blocks, *ordered)
    other = swap(send, "core")
    summed = (keep.astype(F32) + other.astype(F32)).astype(BF16)
    plane = lax.all_to_all(summed, PLANE_GROUP, 0, 0, tiled=True)
    columns = call(plane_kernel, shape(8, 24, 128), scratch=(pltpu.VMEM((BLOCK, 128), F32),))(plane)
    column = lax.all_to_all(columns, COLUMN_GROUP, 0, 0, tiled=True)
    share_in, share_out, share_bias = call(
        functools.partial(column_kernel, 1.0 / math.sqrt(float(tokens))),
        (shape(3, PAIR, dtype=F32), shape(3, PAIR, dtype=F32), shape(1, 3, dtype=F32)),
    )(column)
    features, grads = call(unpack_kernel, (shape(width, rows), shape(width, rows)), smem=1)(me, give_back(back))
    return features.T, grads.T, share_in, share_out, share_bias.reshape(3)


def solution(mesh):
    bits = Mesh(mesh.devices.reshape((2,) * len(BITS)), BITS)
    in_specs = (P(BITS, None), P(BITS, None), P(), P(), P())
    out_specs = (P(BITS, None), P(BITS, None), P(BITS, None), P(BITS, None), P(BITS))
    return jax.shard_map(on_device, mesh=bits, in_specs=in_specs, out_specs=out_specs, check_vma=False)
```
